32 devices in a mesh: groups: 2 (over y), tensor: 4 (over z), req: 2 (over x), pair: 2 (over core).
Axes of the slice: x: 2, y: 2, z: 4, core: 2. Of those that a mesh axis runs over, the one named last changes fastest.
Arguments:
- residual_input: bfloat16 [4, 64, 8192], P(('groups', 'pair'), None, ('req', 'tensor')), parts along dimension 0
- contexts: bfloat16 [2, 4, 64, 8192], P(None, ('groups', 'pair'), 'req', 'tensor'), parts along dimension 1, may hold values from -6 to 6
- projection_weight: bfloat16 [2, 8192, 8192], P(None, 'tensor', 'req'), may hold values from -0.0625 to 0.0625
- adapter_down_factors: bfloat16 [2, 64, 8192, 64], P(None, ('req', 'pair'), 'tensor'), may hold values from -0.0625 to 0.0625
- adapter_up_factors: bfloat16 [2, 64, 64, 8192], P(None, None, None, ('req', 'tensor')), may hold values from -0.75 to 0.75
- norm_gain_vector: bfloat16 [8192], P(('req', 'tensor')), may hold values from 0.5 to 1.5
- request_adapter_index: int32 [4, 64], P('groups'), parts along dimension 0, may hold values from 0 to 63, as said below
Outputs:
- residual_out: bfloat16 [4, 64, 8192], P(('groups', 'pair'), None, ('req', 'tensor')), parts along dimension 0
- normed: bfloat16 [4, 64, 8192], P(('groups', 'pair'), None, ('req', 'tensor')), parts along dimension 0
The draws below stay inside these ranges and needn't reach their ends.
There are 2 independent parts, one for each index of `groups`. The reference program is written for one: setup_inputs(seed, part) draws one part's arguments, and reference() takes and returns one part's arrays. A program takes and returns all parts, laid end to end along the dimension named above; an argument that names none is the same for every part. Nothing has to cross between parts.
Inputs may be any that keep to these rules, and one draw needn't show every extreme that they name: `request_adapter_index`: owner o holds adapters o * 16 to (o + 1) * 16 - 1. The requests r * 32 to (r + 1) * 32 - 1 of one half use exactly 4 different adapters, at most 2 of them held by one owner, and exactly 2 by some owner.
All inputs are finite; a program needn't handle non-finite values.
Results may differ from the reference program's by a relative error of at most 0.0085.
Values may be sent and summed in bfloat16 or wider, within the bound.
A program may use at most 256 MiB of HBM per device.

```python
import jax
import jax.numpy as jnp
from jax import lax

MODEL_WIDTH = 8192
ADAPTER_RANK = 64
ADAPTER_COUNT = 64
DECODER_LAYERS = 2
REQ_DEV = 32
CAP = 2
SLOTS = 4
HALVES = 2
HALF = 64
OWNERS = 4
OWN = 16


def draw_residual_input(key, part):
    key = jax.random.fold_in(key, 11)
    key_base, key_rows, key_cols = jax.random.split(key, 3)
    shape = (HALVES, HALF, MODEL_WIDTH)
    values = jax.random.normal(key_base, shape, jnp.float32)
    row_scale = jnp.exp(jax.random.uniform(key_rows, (HALVES, HALF), jnp.float32, jnp.log(0.25), jnp.log(2.5)))
    ramp = 1.0 + 2.0 * jnp.arange(MODEL_WIDTH, dtype=jnp.float32) / (MODEL_WIDTH - 1)
    col_scale = ramp * jnp.exp(jax.random.uniform(key_cols, (MODEL_WIDTH,), jnp.float32, jnp.log(0.5), jnp.log(2.0)))
    return (values * row_scale[:, :, None] * col_scale[None, None, :]).astype(jnp.bfloat16)


def draw_request_adapter_index(key, part):
    key = jax.random.fold_in(key, 5)
    keys = jax.random.split(key, 7)
    popular = jax.random.permutation(keys[0], OWNERS)
    first = jax.random.randint(keys[1], (OWNERS,), 0, OWNERS)
    second = jax.random.randint(keys[2], (OWNERS,), 0, OWNERS)
    home = popular[jnp.minimum(first, second)]
    home = home.at[0].set(OWNERS - 1).at[1].set(0)
    orders = jax.vmap(lambda sub: jax.random.permutation(sub, OWNERS))(jax.random.split(keys[3], OWNERS))
    others = jax.vmap(lambda row, owner: row[jnp.argsort((row == owner).astype(jnp.int32), stable=True)])(orders, home)
    offsets = jax.random.randint(keys[4], (OWNERS, 2), 0, OWN)
    offsets = offsets.at[0, 0].set(OWN - 1).at[1, 0].set(0)
    steps_home = jnp.arange(CAP, dtype=jnp.int32)
    home_ids = home[:, None] * OWN + (offsets[:, 0:1] + steps_home[None, :]) % OWN
    extra = jnp.arange(SLOTS - CAP, dtype=jnp.int32)
    column = jnp.broadcast_to((extra % (OWNERS - 1))[None, :], (OWNERS, SLOTS - CAP))
    other_owner = jnp.take_along_axis(others, column, axis=1)
    other_ids = other_owner * OWN + (offsets[:, 1:2] + (extra // (OWNERS - 1))[None, :]) % OWN
    plan = jnp.concatenate([home_ids, other_ids], axis=1)
    placed = jax.vmap(lambda sub: jax.random.permutation(sub, REQ_DEV))(jax.random.split(keys[5], OWNERS))
    spare = jax.random.randint(keys[6], (OWNERS, REQ_DEV), 0, SLOTS)
    slot = jnp.where(placed < SLOTS, placed, spare)
    chosen = jnp.take_along_axis(plan, slot, axis=1)
    chosen = chosen.reshape(OWNERS // HALVES, HALVES, REQ_DEV).transpose(1, 0, 2)
    return chosen.reshape(HALVES, HALF).astype(jnp.int32)


def steps_of(key, extent, cuts, least, top_value):
    factor_of = 1.0
    for axis_at, shards_of in cuts:
        steps = jax.random.uniform(jax.random.fold_in(jax.random.fold_in(key, 6), axis_at), (shards_of,), jnp.float32, least / len(cuts), top_value / len(cuts))
        factor_of = factor_of * jnp.repeat(jnp.exp(steps), extent[axis_at] // shards_of).reshape((-1,) + (1,) * (len(extent) - 1 - axis_at))
    return factor_of


def bell_draw(stream_key, shape, deviation, reach, shards=(), kind=jnp.bfloat16):
    array = deviation * jax.random.normal(stream_key, shape, jnp.float32)
    if shards:
        array = array * steps_of(stream_key, shape, shards, -0.22, 0.18)
    return jnp.clip(array, -reach, reach).astype(kind)


def setup_inputs(seed: int = 0, part: int = 0) -> dict:
    arg_keys = jax.random.split(jax.random.key(seed), 8)
    own_keys = jax.random.split(jax.random.fold_in(arg_keys[7], part), 8)
    residual_input = draw_residual_input(jax.random.fold_in(jax.random.fold_in(arg_keys[7], part), 71), part)
    contexts = bell_draw(own_keys[1], (DECODER_LAYERS, HALVES, HALF, MODEL_WIDTH), 1.0, 6.0, ((1, 2), (2, 2), (3, 4)))
    projection_weight = bell_draw(arg_keys[2], (DECODER_LAYERS, MODEL_WIDTH, MODEL_WIDTH), MODEL_WIDTH ** -0.5, 0.0625, ((1, 4), (2, 2)))
    adapter_down_factors = bell_draw(arg_keys[3], (DECODER_LAYERS, ADAPTER_COUNT, MODEL_WIDTH, ADAPTER_RANK), MODEL_WIDTH ** -0.5, 0.0625, ((1, 4), (2, 4)))
    adapter_up_factors = bell_draw(arg_keys[4], (DECODER_LAYERS, ADAPTER_COUNT, ADAPTER_RANK, MODEL_WIDTH), ADAPTER_RANK ** -0.5, 0.75, ((3, 8),))
    norm_gain_vector = jnp.clip(1.0 + 0.1 * jax.random.normal(arg_keys[5], (MODEL_WIDTH,), jnp.float32), 0.5, 1.5).astype(jnp.bfloat16)
    request_adapter_index = draw_request_adapter_index(jax.random.fold_in(jax.random.fold_in(arg_keys[7], part), 71), part)
    return dict(residual_input=residual_input, contexts=contexts, projection_weight=projection_weight, adapter_down_factors=adapter_down_factors, adapter_up_factors=adapter_up_factors, norm_gain_vector=norm_gain_vector, request_adapter_index=request_adapter_index)


adapter_scale = 2.0
norm_eps = 1e-05

def reference(residual_input, contexts, projection_weight, adapter_down_factors, adapter_up_factors, norm_gain_vector, request_adapter_index):
    flat_ids = request_adapter_index.reshape(-1)
    choose = (flat_ids[:, None] == jnp.arange(ADAPTER_COUNT, dtype=jnp.int32)[None, :]).astype(jnp.float32)
    hidden_state = residual_input.reshape(-1, MODEL_WIDTH)
    rows_all = hidden_state.shape[0]
    for layer_number in range(DECODER_LAYERS):
        context = contexts[layer_number].reshape(-1, MODEL_WIDTH)
        base_product = jnp.dot(context, projection_weight[layer_number], preferred_element_type=jnp.float32)
        layer_down_factor = adapter_down_factors[layer_number]
        layer_up_factor = adapter_up_factors[layer_number]

        def shrink_step(total, adapter):
            part = jnp.dot(context, layer_down_factor[adapter], preferred_element_type=jnp.float32)
            return (total + choose[:, adapter][:, None] * part, None)
        shrink_total, _ = lax.scan(shrink_step, jnp.zeros((rows_all, ADAPTER_RANK), jnp.float32), jnp.arange(ADAPTER_COUNT, dtype=jnp.int32))
        shrink = shrink_total.astype(jnp.bfloat16)

        def expand_step(total, adapter):
            part = jnp.dot(shrink, layer_up_factor[adapter], preferred_element_type=jnp.float32)
            return (total + choose[:, adapter][:, None] * part, None)
        expand_product, _ = lax.scan(expand_step, jnp.zeros((rows_all, MODEL_WIDTH), jnp.float32), jnp.arange(ADAPTER_COUNT, dtype=jnp.int32))
        hidden_state = (hidden_state.astype(jnp.float32) + base_product + adapter_scale * expand_product).astype(jnp.bfloat16)
    wide = hidden_state.astype(jnp.float32)
    mean_square = lax.optimization_barrier(jnp.mean(wide * wide, axis=-1))
    normed = wide * lax.rsqrt(mean_square + norm_eps)[:, None] * norm_gain_vector.astype(jnp.float32)[None, :]
    return (hidden_state.reshape(residual_input.shape), normed.astype(jnp.bfloat16).reshape(residual_input.shape))
```

```python
import functools

import jax
import jax.numpy as jnp
from jax import lax
from jax.experimental import pallas as pl
from jax.experimental.pallas import tpu as pltpu
from jax.sharding import PartitionSpec as P

MODEL_WIDTH = 8192
DECODER_LAYERS = 2


adapter_scale = 2.0
norm_eps = 1e-05


def plain_shards(
    residual_input,
    contexts,
    projection_weight,
    adapter_down_factors,
    adapter_up_factors,
    norm_gain_vector,
    request_adapter_index,
):
    req_count = contexts.shape[2]
    half_index = lax.axis_index("pair")
    req_index = lax.axis_index("req")
    index_half_split = lax.dynamic_index_in_dim(
        request_adapter_index, half_index, 0, keepdims=False
    )
    ids_own = lax.dynamic_slice_in_dim(index_half_split, req_index * req_count, req_count, 0)
    hidden_state = residual_input[0]
    for layer_number in range(DECODER_LAYERS):
        context_own = contexts[layer_number, 0]
        context_all = lax.all_gather(context_own, "req", axis=0, tiled=True)
        weight_layer = projection_weight[layer_number]
        base_product = lax.psum_scatter(
            lax.dot_general(
                weight_layer,
                context_all,
                (((0,), (1,)), ((), ())),
                preferred_element_type=jnp.float32,
            ),
            "tensor",
            scatter_dimension=0,
            tiled=True,
        ).T
        layer_down_factor = adapter_down_factors[layer_number]
        whole_pool = lax.all_gather(layer_down_factor, ("req", "pair"), axis=0, tiled=True)
        blocks = whole_pool[ids_own]
        partial_value = jnp.einsum(
            "ik,ikr->ir", context_own, blocks, preferred_element_type=jnp.float32
        )
        shrink_own = lax.psum(partial_value, "tensor").astype(jnp.bfloat16)
        shrink_all = lax.all_gather(shrink_own, "req", axis=0, tiled=True)
        selected_up_factor = adapter_up_factors[layer_number][index_half_split]
        expand_product = jnp.einsum(
            "ir,irc->ic", shrink_all, selected_up_factor, preferred_element_type=jnp.float32
        )
        hidden_state = (
            hidden_state.astype(jnp.float32) + base_product + adapter_scale * expand_product
        ).astype(jnp.bfloat16)
    wide = hidden_state.astype(jnp.float32)
    squares = lax.psum(jnp.sum(wide * wide, axis=-1), ("tensor", "req"))
    mean_square = squares / MODEL_WIDTH
    normed = (
        wide
        * lax.rsqrt(mean_square + norm_eps)[:, None]
        * norm_gain_vector.astype(jnp.float32)[None, :]
    )
    return (hidden_state[None], normed.astype(jnp.bfloat16)[None])


def offsets(sizes):
    t_size, r_size, p_size = sizes
    return [
        (dt, dr, dp)
        for dt in range(t_size)
        for dr in range(r_size)
        for dp in range(p_size)
        if (dt, dr, dp) != (0, 0, 0)
    ]


def fused_kernel(
    sizes,
    res_ref, ctx_ref, w_ref, d_ref, u_ref, gain_ref, ids_ref,
    out_ref, norm_ref,
    wbuf, dbuf, ubuf, cbuf, part, rs_buf, shr, own_sum, zsend, zrecv, delta, swap, sq_buf, sq_recv,
    w_sem, d_sem, u_sem, c_send, c_recv, rs_send, rs_recv, ag_send, ag_recv,
    z_send, z_recv, p_send, p_recv, n_send, n_recv,
):
    t_size, r_size, p_size = sizes
    t = lax.axis_index("tensor")
    r = lax.axis_index("req")
    p = lax.axis_index("pair")
    layers, _, rows_own, k_size = ctx_ref.shape
    half = rows_own * r_size
    rows = half * p_size
    cols = res_ref.shape[2]
    ncol = cols // p_size
    pool = u_ref.shape[1]
    rank = 64

    def dev(dt, dr, dp):
        return {
            "tensor": lax.rem(t + dt, t_size),
            "req": lax.rem(r + dr, r_size),
            "pair": lax.rem(p + dp, p_size),
        }

    def number(d):
        return (d["tensor"] * r_size + d["req"]) * p_size + d["pair"]

    def remote(src, dst, ssem, rsem, target):
        return pltpu.make_async_remote_copy(
            src_ref=src, dst_ref=dst, send_sem=ssem, recv_sem=rsem,
            device_id=target, device_id_type=pl.DeviceIdType.MESH,
        )

    if t_size == 4:
        blocks = [3 - t, lax.rem(t + 2, 4), t + 1 - 2 * lax.rem(t, 2), t]
    else:
        blocks = [lax.rem(t + j + 1, t_size) for j in range(t_size)]

    d_copies = [
        pltpu.make_async_copy(d_ref.at[l], dbuf.at[l], d_sem.at[l]) for l in range(layers)
    ]
    w_copies = [
        [
            pltpu.make_async_copy(
                w_ref.at[l, :, pl.ds(pl.multiple_of(blocks[j] * cols + p * ncol, ncol), ncol)],
                wbuf.at[j, l],
                w_sem.at[j, l],
            )
            for l in range(layers)
        ]
        for j in range(t_size)
    ]
    u_copies = [
        pltpu.make_async_copy(
            u_ref.at[l, :, pl.ds(pl.multiple_of(p * ncol, ncol), ncol)], ubuf.at[l], u_sem.at[l]
        )
        for l in range(layers)
    ]
    for c in d_copies:
        c.start()
    for js in w_copies:
        for c in js:
            c.start()
    for c in u_copies:
        c.start()

    barrier = pltpu.get_barrier_semaphore()
    offs = offsets(sizes)
    for o in offs:
        pl.semaphore_signal(
            barrier, inc=1, device_id=dev(*o), device_id_type=pl.DeviceIdType.MESH
        )
    pl.semaphore_wait(barrier, len(offs))

    row_own = pl.multiple_of(p * half + r * rows_own, rows_own)
    row_far = pl.multiple_of(p * half + (1 - r) * rows_own, rows_own)
    x_copies, m_copies, f_copies = [], [], []
    for l in range(layers):
        x_copies.append(remote(
            ctx_ref.at[l, 0], cbuf.at[l, pl.ds(row_own, rows_own)],
            c_send.at[0, l], c_recv.at[0, l], dev(0, 1, 0)))
        m_copies.append(remote(
            ctx_ref.at[l, 0], cbuf.at[l, pl.ds(row_own, rows_own)],
            c_send.at[1, l], c_recv.at[1, l], dev(0, 0, 1)))
        f_copies.append(remote(
            cbuf.at[l, pl.ds(row_far, rows_own)], cbuf.at[l, pl.ds(row_far, rows_own)],
            c_send.at[2, l], c_recv.at[2, l], dev(0, 0, 1)))
    for c in x_copies:
        c.start()
    for c in m_copies:
        c.start()
    for l in range(layers):
        cbuf[l, pl.ds(row_own, rows_own), :] = ctx_ref[l, 0]

    lane = lax.broadcasted_iota(jnp.int32, (rows, 128), 1)
    low = lane < rank
    upper = jnp.where(low, 0, 1)
    id_rows = ids_ref[...].astype(jnp.float32)
    id_row = jnp.concatenate([id_rows[h : h + 1] for h in range(p_size)], axis=1)
    id_mat = jnp.broadcast_to(id_row, (rows, rows)).T.astype(jnp.int32)

    for l in range(layers):
        x_copies[l].wait_recv()
        f_copies[l].start()
    for l in range(layers):
        m_copies[l].wait_recv()
        f_copies[l].wait_recv()

    own_base = (r * p_size + p) * (dbuf.shape[1] // rank)
    folded = []
    for l in range(layers):
        d_copies[l].wait()
        wide = lax.dot_general(
            cbuf[l], dbuf[l], (((1,), (1,)), ((), ())), preferred_element_type=jnp.float32
        )
        total = jnp.zeros((rows, 128), jnp.float32)
        for k in range(dbuf.shape[1] // 128):
            use = id_mat == own_base + 2 * k + upper
            total = total + jnp.where(use, wide[:, k * 128 : (k + 1) * 128], 0.0)
        folded.append(total + pltpu.roll(total, rank, 1))
    part[...] = jnp.where(low, folded[0], folded[1])

    me = {"tensor": t, "req": r, "pair": p}
    mine = number(me)
    piece = part.shape[0] // (len(offs) + 1)
    rs_copies = []
    for i, o in enumerate(offs):
        target = dev(*o)
        c = remote(
            part.at[pl.ds(pl.multiple_of(number(target) * piece, piece), piece)],
            rs_buf.at[i], rs_send.at[i], rs_recv.at[i], target)
        c.start()
        rs_copies.append(c)

    def project(j):
        acc = None
        for l in range(layers):
            w_copies[j][l].wait()
            term = jnp.dot(cbuf[l], wbuf[j, l], preferred_element_type=jnp.float32)
            acc = term if acc is None else acc + term
        return acc

    z_copies = []

    def project_and_send(j):
        zsend[j] = project(j).astype(jnp.bfloat16)
        target = {"tensor": blocks[j], "req": r, "pair": p}
        c = remote(zsend.at[j], zrecv.at[j], z_send.at[j], z_recv.at[j], target)
        c.start()
        z_copies.append(c)

    project_and_send(0)

    for c in rs_copies:
        c.wait_recv()
    at_mine = pl.ds(pl.multiple_of(mine * piece, piece), piece)
    total = part[at_mine, :]
    for i in range(len(offs)):
        total = total + rs_buf[i]
    shr[at_mine, :] = total.astype(jnp.bfloat16).astype(jnp.float32)
    ag_copies = []
    for i, o in enumerate(offs):
        c = remote(shr.at[at_mine], shr.at[at_mine], ag_send.at[i], ag_recv.at[i], dev(*o))
        c.start()
        ag_copies.append(c)

    for j in range(1, t_size - 1):
        project_and_send(j)
    own_sum[...] = project(t_size - 1)

    for i in range(len(offs)):
        ag_copies[i].wait_recv()
    shrink = shr[...]
    other = pltpu.roll(shrink, rank, 1)
    expand = None
    for l in range(layers):
        u_copies[l].wait()
        both = jnp.where(low, shrink, other) if l == 0 else jnp.where(low, other, shrink)
        placed = jnp.concatenate(
            [
                jnp.where(id_mat == 2 * k + upper, both, 0.0).astype(jnp.bfloat16)
                for k in range(pool // 128)
            ],
            axis=1,
        )
        term = jnp.dot(placed, ubuf[l], preferred_element_type=jnp.float32)
        expand = term if expand is None else expand + term
    own_sum[...] += adapter_scale * expand

    for c in z_copies:
        c.wait_recv()
    acc = own_sum[...]
    for j in range(t_size - 1):
        acc = acc + zrecv[j].astype(jnp.float32)
    delta[...] = acc

    give = pl.ds(pl.multiple_of((1 - p) * half, half), half)
    keep = pl.ds(pl.multiple_of(p * half, half), half)
    swap_copy = remote(
        delta.at[give], swap, p_send.at[0], p_recv.at[0], dev(0, 0, 1))
    swap_copy.start()
    swap_copy.wait_recv()
    kept, got = delta[keep, :], swap[...]
    first = p == 0
    left = jnp.where(first, kept, got)
    right = jnp.where(first, got, kept)
    hidden = []
    for q, add in enumerate((left, right)):
        at = slice(q * ncol, (q + 1) * ncol)
        value = (res_ref[0, :, at].astype(jnp.float32) + add).astype(jnp.bfloat16)
        out_ref[0, :, at] = value
        hidden.append(value.astype(jnp.float32))
    sq = jnp.zeros((half, 128), jnp.float32)
    for value in hidden:
        for k in range(ncol // 128):
            tile = value[:, k * 128 : (k + 1) * 128]
            sq = sq + tile * tile
    padded = jnp.concatenate([sq, jnp.zeros((128 - half, 128), jnp.float32)], axis=0) if half < 128 else sq
    sq_row = jnp.sum(padded.T, axis=0, keepdims=True)
    sq_buf[...] = jnp.broadcast_to(sq_row, sq_buf.shape)
    n_copies = []
    n_offs = [o for o in offs if o[2] == 0]
    for i, o in enumerate(n_offs):
        c = remote(sq_buf, sq_recv.at[i], n_send.at[i], n_recv.at[i], dev(*o))
        c.start()
        n_copies.append(c)
    for c in n_copies:
        c.wait_recv()
    sums = sq_buf[...]
    for i in range(len(n_offs)):
        sums = sums + sq_recv[i]
    inverse = lax.rsqrt(sums[0:1] / MODEL_WIDTH + norm_eps)
    scale = jnp.broadcast_to(inverse, (128, 128)).T[:half]
    for q, value in enumerate(hidden):
        for k in range(ncol // 128):
            at = q * ncol + k * 128
            g = gain_ref[at // 128 : at // 128 + 1, :].astype(jnp.float32)
            tile = value[:, k * 128 : (k + 1) * 128]
            norm_ref[0, :, at : at + 128] = (tile * scale * g).astype(jnp.bfloat16)

    for group in (x_copies, m_copies, f_copies, rs_copies, ag_copies, z_copies, [swap_copy], n_copies):
        for c in group:
            c.wait_send()


def fits(sizes, residual_input, contexts, adapter_down_factors, adapter_up_factors):
    t_size, r_size, p_size = sizes
    layers, _, rows_own, k_size = contexts.shape
    rows = rows_own * r_size * p_size
    rank = adapter_down_factors.shape[3]
    return (
        t_size == 4 and r_size == 2 and p_size == 2 and layers == 2 and rows == 128
        and rank == 64 and rows_own % 16 == 0 and residual_input.shape[2] % 256 == 0
        and adapter_up_factors.shape[1] % 2 == 0 and adapter_down_factors.shape[1] % 2 == 0
        and k_size % 128 == 0
    )


def shards(sizes, *args):
    (residual_input, contexts, projection_weight, adapter_down_factors, adapter_up_factors,
     norm_gain_vector, request_adapter_index) = args
    if not fits(sizes, residual_input, contexts, adapter_down_factors, adapter_up_factors):
        return plain_shards(*args)
    t_size, r_size, p_size = sizes
    layers, _, rows_own, k_size = contexts.shape
    half = rows_own * r_size
    rows = half * p_size
    cols = residual_input.shape[2]
    ncol = cols // p_size
    own, rank = adapter_down_factors.shape[1], adapter_down_factors.shape[3]
    down = jnp.swapaxes(adapter_down_factors, 2, 3).reshape(layers, own * rank, k_size)
    pool = adapter_up_factors.shape[1] * rank
    up = adapter_up_factors.reshape(layers, pool, cols)
    gain = norm_gain_vector.reshape(cols // 128, 128)
    peers = t_size * r_size * p_size - 1
    n_peers = t_size * r_size - 1
    piece = rows // (peers + 1)
    vmem = pl.BlockSpec(memory_space=pltpu.VMEM)
    hbm = pl.BlockSpec(memory_space=pl.ANY)
    dma = pltpu.SemaphoreType.DMA
    return pl.pallas_call(
        functools.partial(fused_kernel, sizes),
        out_shape=(
            jax.ShapeDtypeStruct(residual_input.shape, jnp.bfloat16),
            jax.ShapeDtypeStruct(residual_input.shape, jnp.bfloat16),
        ),
        in_specs=[vmem, vmem, hbm, hbm, hbm, vmem, vmem],
        out_specs=(vmem, vmem),
        scratch_shapes=[
            pltpu.VMEM((t_size, layers, k_size, ncol), jnp.bfloat16),
            pltpu.VMEM((layers, own * rank, k_size), jnp.bfloat16),
            pltpu.VMEM((layers, pool, ncol), jnp.bfloat16),
            pltpu.VMEM((layers, rows, k_size), jnp.bfloat16),
            pltpu.VMEM((rows, 128), jnp.float32),
            pltpu.VMEM((peers, piece, 128), jnp.float32),
            pltpu.VMEM((rows, 128), jnp.float32),
            pltpu.VMEM((rows, ncol), jnp.float32),
            pltpu.VMEM((t_size - 1, rows, ncol), jnp.bfloat16),
            pltpu.VMEM((t_size - 1, rows, ncol), jnp.bfloat16),
            pltpu.VMEM((rows, ncol), jnp.float32),
            pltpu.VMEM((half, ncol), jnp.float32),
            pltpu.VMEM((8, 128), jnp.float32),
            pltpu.VMEM((n_peers, 8, 128), jnp.float32),
            dma((t_size, layers)), dma((layers,)), dma((layers,)),
            dma((3, layers)), dma((3, layers)),
            dma((peers,)), dma((peers,)), dma((peers,)), dma((peers,)),
            dma((t_size - 1,)), dma((t_size - 1,)),
            dma((1,)), dma((1,)), dma((n_peers,)), dma((n_peers,)),
        ],
        compiler_params=pltpu.CompilerParams(
            collective_id=0, has_side_effects=True, vmem_limit_bytes=48 * 1024 * 1024
        ),
    )(residual_input, contexts, projection_weight, down, up, gain, request_adapter_index)


def solution(mesh):
    sizes = (mesh.shape["tensor"], mesh.shape["req"], mesh.shape["pair"])
    in_specs = (
        P(("groups", "pair"), None, ("req", "tensor")),
        P(None, ("groups", "pair"), "req", "tensor"),
        P(None, "tensor", "req"),
        P(None, ("req", "pair"), "tensor", None),
        P(None, None, None, ("req", "tensor")),
        P(("req", "tensor")),
        P("groups", None),
    )
    out_specs = (
        P(("groups", "pair"), None, ("req", "tensor")),
        P(("groups", "pair"), None, ("req", "tensor")),
    )
    return jax.shard_map(functools.partial(shards, sizes), mesh=mesh, in_specs=in_specs, out_specs=out_specs, check_vma=False)
```

```python
import functools

import jax
import jax.numpy as jnp
from jax import lax
from jax.experimental import pallas as pl
from jax.experimental.pallas import tpu as pltpu
from jax.sharding import PartitionSpec as P

MODEL_WIDTH = 8192
DECODER_LAYERS = 2


adapter_scale = 2.0
norm_eps = 1e-05


def plain_shards(
    residual_input,
    contexts,
    projection_weight,
    adapter_down_factors,
    adapter_up_factors,
    norm_gain_vector,
    request_adapter_index,
):
    req_count = contexts.shape[2]
    half_index = lax.axis_index("pair")
    req_index = lax.axis_index("req")
    index_half_split = lax.dynamic_index_in_dim(
        request_adapter_index, half_index, 0, keepdims=False
    )
    ids_own = lax.dynamic_slice_in_dim(index_half_split, req_index * req_count, req_count, 0)
    hidden_state = residual_input[0]
    for layer_number in range(DECODER_LAYERS):
        context_own = contexts[layer_number, 0]
        context_all = lax.all_gather(context_own, "req", axis=0, tiled=True)
        weight_layer = projection_weight[layer_number]
        base_product = lax.psum_scatter(
            lax.dot_general(
                weight_layer,
                context_all,
                (((0,), (1,)), ((), ())),
                preferred_element_type=jnp.float32,
            ),
            "tensor",
            scatter_dimension=0,
            tiled=True,
        ).T
        layer_down_factor = adapter_down_factors[layer_number]
        whole_pool = lax.all_gather(layer_down_factor, ("req", "pair"), axis=0, tiled=True)
        blocks = whole_pool[ids_own]
        partial_value = jnp.einsum(
            "ik,ikr->ir", context_own, blocks, preferred_element_type=jnp.float32
        )
        shrink_own = lax.psum(partial_value, "tensor").astype(jnp.bfloat16)
        shrink_all = lax.all_gather(shrink_own, "req", axis=0, tiled=True)
        selected_up_factor = adapter_up_factors[layer_number][index_half_split]
        expand_product = jnp.einsum(
            "ir,irc->ic", shrink_all, selected_up_factor, preferred_element_type=jnp.float32
        )
        hidden_state = (
            hidden_state.astype(jnp.float32) + base_product + adapter_scale * expand_product
        ).astype(jnp.bfloat16)
    wide = hidden_state.astype(jnp.float32)
    squares = lax.psum(jnp.sum(wide * wide, axis=-1), ("tensor", "req"))
    mean_square = squares / MODEL_WIDTH
    normed = (
        wide
        * lax.rsqrt(mean_square + norm_eps)[:, None]
        * norm_gain_vector.astype(jnp.float32)[None, :]
    )
    return (hidden_state[None], normed.astype(jnp.bfloat16)[None])


def offsets(sizes):
    t_size, r_size, p_size = sizes
    return [
        (dt, dr, dp)
        for dt in range(t_size)
        for dr in range(r_size)
        for dp in range(p_size)
        if (dt, dr, dp) != (0, 0, 0)
    ]


def fused_kernel(
    sizes,
    res_ref, ctx_ref, w_ref, d_ref, u_ref, gain_ref, ids_ref,
    out_ref, norm_ref,
    res_buf, gain_buf, id_buf, id_buf_wide,
    wbuf, dbuf, ubuf, cbuf, part, rs_buf, shr, own_sum, zsend, zrecv, delta, swap, sq_buf, sq_recv,
    in_sem, w_sem, d_sem, u_sem, c_send, c_recv, rs_send, rs_recv, ag_send, ag_recv,
    z_send, z_recv, p_send, p_recv, n_send, n_recv,
):
    t_size, r_size, p_size = sizes
    t = lax.axis_index("tensor")
    r = lax.axis_index("req")
    p = lax.axis_index("pair")
    layers, _, rows_own, k_size = ctx_ref.shape
    half = rows_own * r_size
    rows = half * p_size
    cols = res_buf.shape[2]
    ncol = cols // p_size
    pool = u_ref.shape[1]
    rank = 64

    def dev(dt, dr, dp):
        return {
            "tensor": lax.rem(t + dt, t_size),
            "req": lax.rem(r + dr, r_size),
            "pair": lax.rem(p + dp, p_size),
        }

    def number(d):
        return (d["tensor"] * r_size + d["req"]) * p_size + d["pair"]

    def remote(src, dst, ssem, rsem, target):
        return pltpu.make_async_remote_copy(
            src_ref=src, dst_ref=dst, send_sem=ssem, recv_sem=rsem,
            device_id=target, device_id_type=pl.DeviceIdType.MESH,
        )

    if t_size == 4:
        blocks = [3 - t, lax.rem(t + 2, 4), t + 1 - 2 * lax.rem(t, 2), t]
    else:
        blocks = [lax.rem(t + j + 1, t_size) for j in range(t_size)]

    d_copies = [
        pltpu.make_async_copy(d_ref.at[l], dbuf.at[l], d_sem.at[l]) for l in range(layers)
    ]
    w_copies = [
        [
            pltpu.make_async_copy(
                w_ref.at[l, :, pl.ds(pl.multiple_of(blocks[j] * cols + p * ncol, ncol), ncol)],
                wbuf.at[j, l],
                w_sem.at[j, l],
            )
            for l in range(layers)
        ]
        for j in range(t_size)
    ]
    u_copies = [
        pltpu.make_async_copy(
            u_ref.at[l, :, pl.ds(pl.multiple_of(p * ncol, ncol), ncol)], ubuf.at[l], u_sem.at[l]
        )
        for l in range(layers)
    ]
    row_own = pl.multiple_of(r * 2 * rows_own + p * rows_own, rows_own)
    row_far = pl.multiple_of((1 - r) * 2 * rows_own + p * rows_own, rows_own)
    own_copies = [
        pltpu.make_async_copy(ctx_ref.at[l, 0], cbuf.at[l, pl.ds(row_own, rows_own)], in_sem.at[l])
        for l in range(layers)
    ]
    small_copies = [
        pltpu.make_async_copy(ids_ref, id_buf, in_sem.at[layers]),
        pltpu.make_async_copy(res_ref, res_buf, in_sem.at[layers + 1]),
        pltpu.make_async_copy(gain_ref, gain_buf, in_sem.at[layers + 2]),
    ]
    for c in own_copies + small_copies[:1]:
        c.start()
    for js in w_copies[:-1]:
        for c in js:
            c.start()
    for c in d_copies + w_copies[-1] + u_copies + small_copies[1:]:
        c.start()

    barrier = pltpu.get_barrier_semaphore()
    offs = offsets(sizes)
    for o in offs:
        pl.semaphore_signal(
            barrier, inc=1, device_id=dev(*o), device_id_type=pl.DeviceIdType.MESH
        )
    pl.semaphore_wait(barrier, len(offs))

    x_copies, m_copies, f_copies = [], [], []
    for l in range(layers):
        x_copies.append(remote(
            ctx_ref.at[l, 0], cbuf.at[l, pl.ds(row_own, rows_own)],
            c_send.at[0, l], c_recv.at[0, l], dev(0, 1, 0)))
        m_copies.append(remote(
            ctx_ref.at[l, 0], cbuf.at[l, pl.ds(row_own, rows_own)],
            c_send.at[1, l], c_recv.at[1, l], dev(0, 0, 1)))
        f_copies.append(remote(
            cbuf.at[l, pl.ds(row_far, rows_own)], cbuf.at[l, pl.ds(row_far, rows_own)],
            c_send.at[2, l], c_recv.at[2, l], dev(0, 0, 1)))
    for c in m_copies:
        c.start()
    for c in x_copies:
        c.start()

    lane = lax.broadcasted_iota(jnp.int32, (rows, 128), 1)
    low = lane < rank
    upper = jnp.where(low, 0, 1)
    small_copies[0].wait()
    id_rows = id_buf[...].astype(jnp.float32)
    id_row = jnp.concatenate(
        [
            id_rows[h : h + 1, q * rows_own : (q + 1) * rows_own]
            for q in range(r_size)
            for h in range(p_size)
        ],
        axis=1,
    )
    id_mat = jnp.broadcast_to(id_row, (rows, rows)).T.astype(jnp.int32)

    near = pl.ds(pl.multiple_of(r * half, half), half)
    far = pl.ds(pl.multiple_of((1 - r) * half, half), half)

    def project(j, at, first):
        acc = None
        for l in range(layers):
            if first:
                w_copies[j][l].wait()
            term = jnp.dot(cbuf[l, at, :], wbuf[j, l], preferred_element_type=jnp.float32)
            acc = term if acc is None else acc + term
        return acc

    z_copies = []

    outer = lax.rem(t // 2 + lax.rem(t, 2) + 1, 2)
    near_t = t + 1 - 2 * lax.rem(t, 2)
    relay = t_size - 1

    def z_copy(j, at, side):
        slot, target = j, blocks[j]
        if j == 0:
            slot = outer * relay
            target = outer * near_t + (1 - outer) * blocks[0]
        return remote(
            zsend.at[j, at], zrecv.at[slot, at], z_send.at[side, j], z_recv.at[side, slot],
            {"tensor": target, "req": r, "pair": p})

    def arrived(j, at, side):
        return remote(
            zsend.at[0, at], zrecv.at[j, at], z_send.at[side, 0], z_recv.at[side, j],
            {"tensor": near_t, "req": r, "pair": p})

    def project_and_send(j, at, side):
        value = project(j, at, side == 0)
        if j == 1:
            own_sum[at, :] = value

            @pl.when(outer == 0)
            def _():
                arrived(relay, at, side).wait_recv()
                own_sum[at, :] += zrecv[relay, at, :].astype(jnp.float32)

            value = own_sum[at, :]
        zsend[j, at, :] = value.astype(jnp.bfloat16)
        c = z_copy(j, at, side)
        c.start()
        z_copies.append(c)

    own_base = (r * p_size + p) * (dbuf.shape[1] // rank)
    id_buf_wide[...] = id_mat

    def shrink_rows(at):
        low_half = low[:half]
        ids_at = id_buf_wide[at, :]
        folded = []
        for l in range(layers):
            wide = lax.dot_general(
                cbuf[l, at, :], dbuf[l], (((1,), (1,)), ((), ())),
                preferred_element_type=jnp.float32,
            )
            total = jnp.zeros((half, 128), jnp.float32)
            for k in range(dbuf.shape[1] // 128):
                use = ids_at == own_base + 2 * k + upper[:half]
                total = total + jnp.where(use, wide[:, k * 128 : (k + 1) * 128], 0.0)
            folded.append(total + pltpu.roll(total, rank, 1))
        part[at, :] = jnp.where(low_half, folded[0], folded[1])

    for l in range(layers):
        own_copies[l].wait()
        m_copies[l].wait_recv()
    for j in (0, 2, 1):
        project_and_send(j, near, 0)
        if j == 0:
            x_copies[0].wait_recv()
            f_copies[0].start()
    x_copies[1].wait_recv()
    f_copies[1].start()
    for c in d_copies:
        c.wait()
    shrink_rows(near)
    for l in range(layers):
        f_copies[l].wait_recv()
    shrink_rows(far)

    me = {"tensor": t, "req": r, "pair": p}
    mine = number(me)
    piece = part.shape[0] // (len(offs) + 1)
    rs_copies = []
    for i, o in enumerate(offs):
        target = dev(*o)
        c = remote(
            part.at[pl.ds(pl.multiple_of(number(target) * piece, piece), piece)],
            rs_buf.at[i], rs_send.at[i], rs_recv.at[i], target)
        c.start()
        rs_copies.append(c)

    project_and_send(0, far, 1)

    for c in rs_copies:
        c.wait_recv()
    at_mine = pl.ds(pl.multiple_of(mine * piece, piece), piece)
    total = part[at_mine, :]
    for i in range(len(offs)):
        total = total + rs_buf[i]
    shr[at_mine, :] = total.astype(jnp.bfloat16).astype(jnp.float32)
    ag_copies = []
    for i, o in enumerate(offs):
        c = remote(shr.at[at_mine], shr.at[at_mine], ag_send.at[i], ag_recv.at[i], dev(*o))
        c.start()
        ag_copies.append(c)

    for j in (2, 1):
        project_and_send(j, far, 1)
    own_sum[...] = project(t_size - 1, slice(None), True)

    for i in range(len(offs)):
        ag_copies[i].wait_recv()
    shrink = shr[...]
    other = pltpu.roll(shrink, rank, 1)
    expand = None
    for l in range(layers):
        u_copies[l].wait()
        both = jnp.where(low, shrink, other) if l == 0 else jnp.where(low, other, shrink)
        placed = jnp.concatenate(
            [
                jnp.where(id_mat == 2 * k + upper, both, 0.0).astype(jnp.bfloat16)
                for k in range(pool // 128)
            ],
            axis=1,
        )
        term = jnp.dot(placed, ubuf[l], preferred_element_type=jnp.float32)
        expand = term if expand is None else expand + term
    own_sum[...] += adapter_scale * expand

    for side, at in enumerate((near, far)):
        for j in (1, 2):
            arrived(j, at, side).wait_recv()

        @pl.when(outer == 0)
        def _():
            arrived(0, at, side).wait_recv()
            own_sum[at, :] += zrecv[0, at, :].astype(jnp.float32)

    acc = own_sum[...]
    for j in (1, 2):
        acc = acc + zrecv[j].astype(jnp.float32)
    delta[...] = acc

    swap_copies = []
    for q in range(r_size):
        give = pl.ds(pl.multiple_of(q * half + (1 - p) * rows_own, rows_own), rows_own)
        c = remote(
            delta.at[give], swap.at[pl.ds(q * rows_own, rows_own)],
            p_send.at[q], p_recv.at[q], dev(0, 0, 1))
        c.start()
        swap_copies.append(c)
    kept = jnp.concatenate(
        [
            delta[pl.ds(pl.multiple_of(q * half + p * rows_own, rows_own), rows_own), :]
            for q in range(r_size)
        ],
        axis=0,
    )
    for c in small_copies[1:]:
        c.wait()
    for c in swap_copies:
        c.wait_recv()
    got = swap[...]
    first = p == 0
    left = jnp.where(first, kept, got)
    right = jnp.where(first, got, kept)
    hidden = []
    for q, add in enumerate((left, right)):
        at = slice(q * ncol, (q + 1) * ncol)
        value = (res_buf[0, :, at].astype(jnp.float32) + add).astype(jnp.bfloat16)
        out_ref[0, :, at] = value
        hidden.append(value.astype(jnp.float32))
    sq = jnp.zeros((half, 128), jnp.float32)
    for value in hidden:
        for k in range(ncol // 128):
            tile = value[:, k * 128 : (k + 1) * 128]
            sq = sq + tile * tile
    padded = jnp.concatenate([sq, jnp.zeros((128 - half, 128), jnp.float32)], axis=0) if half < 128 else sq
    sq_row = jnp.sum(padded.T, axis=0, keepdims=True)
    sq_buf[...] = jnp.broadcast_to(sq_row, sq_buf.shape)
    n_copies = []
    n_offs = [o for o in offs if o[2] == 0]
    for i, o in enumerate(n_offs):
        c = remote(sq_buf, sq_recv.at[i], n_send.at[i], n_recv.at[i], dev(*o))
        c.start()
        n_copies.append(c)
    for c in n_copies:
        c.wait_recv()
    sums = sq_buf[...]
    for i in range(len(n_offs)):
        sums = sums + sq_recv[i]
    inverse = lax.rsqrt(sums[0:1] / MODEL_WIDTH + norm_eps)
    scale = jnp.broadcast_to(inverse, (128, 128)).T[:half]
    for q, value in enumerate(hidden):
        for k in range(ncol // 128):
            at = q * ncol + k * 128
            g = gain_buf[at // 128 : at // 128 + 1, :].astype(jnp.float32)
            tile = value[:, k * 128 : (k + 1) * 128]
            norm_ref[0, :, at : at + 128] = (tile * scale * g).astype(jnp.bfloat16)

    for group in (x_copies, m_copies, f_copies, rs_copies, ag_copies, z_copies, swap_copies, n_copies):
        for c in group:
            c.wait_send()


def fits(sizes, residual_input, contexts, adapter_down_factors, adapter_up_factors):
    t_size, r_size, p_size = sizes
    layers, _, rows_own, k_size = contexts.shape
    rows = rows_own * r_size * p_size
    rank = adapter_down_factors.shape[3]
    return (
        t_size == 4 and r_size == 2 and p_size == 2 and layers == 2 and rows == 128
        and rank == 64 and rows_own % 16 == 0 and residual_input.shape[2] % 256 == 0
        and adapter_up_factors.shape[1] % 2 == 0 and adapter_down_factors.shape[1] % 2 == 0
        and k_size % 128 == 0
    )


def shards(sizes, *args):
    (residual_input, contexts, projection_weight, adapter_down_factors, adapter_up_factors,
     norm_gain_vector, request_adapter_index) = args
    if not fits(sizes, residual_input, contexts, adapter_down_factors, adapter_up_factors):
        return plain_shards(*args)
    t_size, r_size, p_size = sizes
    layers, _, rows_own, k_size = contexts.shape
    half = rows_own * r_size
    rows = half * p_size
    cols = residual_input.shape[2]
    ncol = cols // p_size
    own, rank = adapter_down_factors.shape[1], adapter_down_factors.shape[3]
    down = jnp.swapaxes(adapter_down_factors, 2, 3).reshape(layers, own * rank, k_size)
    pool = adapter_up_factors.shape[1] * rank
    up = adapter_up_factors.reshape(layers, pool, cols)
    gain = norm_gain_vector.reshape(cols // 128, 128)
    peers = t_size * r_size * p_size - 1
    n_peers = t_size * r_size - 1
    piece = rows // (peers + 1)
    vmem = pl.BlockSpec(memory_space=pltpu.VMEM)
    hbm = pl.BlockSpec(memory_space=pltpu.HBM)
    dma = pltpu.SemaphoreType.DMA
    return pl.pallas_call(
        functools.partial(fused_kernel, sizes),
        out_shape=(
            jax.ShapeDtypeStruct(residual_input.shape, jnp.bfloat16),
            jax.ShapeDtypeStruct(residual_input.shape, jnp.bfloat16),
        ),
        in_specs=[hbm] * 7,
        out_specs=(vmem, vmem),
        scratch_shapes=[
            pltpu.VMEM(residual_input.shape, jnp.bfloat16),
            pltpu.VMEM(gain.shape, jnp.bfloat16),
            pltpu.VMEM(request_adapter_index.shape, jnp.int32),
            pltpu.VMEM((rows, 128), jnp.int32),
            pltpu.VMEM((t_size, layers, k_size, ncol), jnp.bfloat16),
            pltpu.VMEM((layers, own * rank, k_size), jnp.bfloat16),
            pltpu.VMEM((layers, pool, ncol), jnp.bfloat16),
            pltpu.VMEM((layers, rows, k_size), jnp.bfloat16),
            pltpu.VMEM((rows, 128), jnp.float32),
            pltpu.VMEM((peers, piece, 128), jnp.float32),
            pltpu.VMEM((rows, 128), jnp.float32),
            pltpu.VMEM((rows, ncol), jnp.float32),
            pltpu.VMEM((t_size - 1, rows, ncol), jnp.bfloat16),
            pltpu.VMEM((t_size, rows, ncol), jnp.bfloat16),
            pltpu.VMEM((rows, ncol), jnp.float32),
            pltpu.VMEM((half, ncol), jnp.float32),
            pltpu.VMEM((8, 128), jnp.float32),
            pltpu.VMEM((n_peers, 8, 128), jnp.float32),
            dma((layers + 3,)), dma((t_size, layers)), dma((layers,)), dma((layers,)),
            dma((3, layers)), dma((3, layers)),
            dma((peers,)), dma((peers,)), dma((peers,)), dma((peers,)),
            dma((2, t_size - 1)), dma((2, t_size)),
            dma((r_size,)), dma((r_size,)), dma((n_peers,)), dma((n_peers,)),
        ],
        compiler_params=pltpu.CompilerParams(
            collective_id=0, has_side_effects=True, vmem_limit_bytes=62 * 1024 * 1024
        ),
    )(residual_input, contexts, projection_weight, down, up, gain, request_adapter_index)


def solution(mesh):
    sizes = (mesh.shape["tensor"], mesh.shape["req"], mesh.shape["pair"])
    in_specs = (
        P(("groups", "pair"), None, ("req", "tensor")),
        P(None, ("groups", "pair"), "req", "tensor"),
        P(None, "tensor", "req"),
        P(None, ("req", "pair"), "tensor", None),
        P(None, None, None, ("req", "tensor")),
        P(("req", "tensor")),
        P("groups", None),
    )
    out_specs = (
        P(("groups", "pair"), None, ("req", "tensor")),
        P(("groups", "pair"), None, ("req", "tensor")),
    )
    return jax.shard_map(functools.partial(shards, sizes), mesh=mesh, in_specs=in_specs, out_specs=out_specs, check_vma=False)
```
